512 devices in a mesh: ctx: 128 (over z, y, core), tp: 4 (over x).
Axes of the slice: x: 4, y: 8, z: 8, core: 2. Of those that a mesh axis runs over, the one named last changes fastest.
Arguments:
- queries: bfloat16 [65536, 4096], P('ctx', 'tp'), may hold values from -9 to 9
- keys: bfloat16 [65536, 512], P('ctx', 'tp'), may hold values from -9 to 9
- values: bfloat16 [65536, 512], P('ctx', 'tp'), may hold values from -6 to 6
- output_gradient: bfloat16 [65536, 4096], P('ctx', 'tp'), may hold values from -6 to 6
- doc_start: int32 [65536], P('ctx'), may hold values from 0 to 65535, as said below
Outputs:
- attended: bfloat16 [65536, 4096], P(('ctx', 'tp'))
- query_gradient: bfloat16 [65536, 4096], P('ctx', 'tp')
- key_gradient: bfloat16 [65536, 512], P('ctx', 'tp')
- value_gradient: bfloat16 [65536, 512], P('ctx', 'tp')
The draws below stay inside these ranges and needn't reach their ends.
Inputs may be any that keep to these rules, and one draw needn't show every extreme that they name: doc_start[i] is the first position of the document holding position i; it never falls along the sequence, and no document crosses a multiple of 512. The shards of 512 positions are matched in pairs, shard s with shard s plus half the number of shards: documents in one of a pair are cut at a rate complementary to the other's, so a shard of long documents is matched with a shard of short ones.
All inputs are finite; a program needn't handle non-finite values.
Results may differ from the reference program's by a relative error of at most 0.025.
Values may be sent and summed in bfloat16 or wider, within the bound.
A program may use at most 64 MiB of HBM per device.

```python
import math
import jax
import jax.numpy as jnp
from jax import lax

HEAD_SIZE = 128
QUERY_HEADS = 32
KEY_VALUE_HEADS = 4
TOKENS_PER_SHARD = 512
PACKED_TOKENS = 65536
N_CTX = 128


def draw_queries(key, part):
    key = jax.random.fold_in(key, 11)
    group_width = QUERY_HEADS // KEY_VALUE_HEADS
    final_result = jnp.clip(jax.random.normal(key, (PACKED_TOKENS, KEY_VALUE_HEADS, group_width, HEAD_SIZE), jnp.float32), -4.0, 4.0)
    return final_result.reshape(PACKED_TOKENS, QUERY_HEADS * HEAD_SIZE).astype(jnp.bfloat16)


def draw_keys(key, part):
    key = jax.random.fold_in(key, 23)
    final_result = jnp.clip(jax.random.normal(key, (PACKED_TOKENS, KEY_VALUE_HEADS, HEAD_SIZE), jnp.float32), -4.0, 4.0)
    return final_result.reshape(PACKED_TOKENS, KEY_VALUE_HEADS * HEAD_SIZE).astype(jnp.bfloat16)


def draw_doc_start(key, part):
    key = jax.random.fold_in(key, 5)
    first_position, second = jax.random.split(key)
    lower = jax.random.randint(first_position, (N_CTX // 2, 1), 0, 9)
    level = jnp.concatenate((lower, 8 - lower), axis=0)
    rolled = jax.random.randint(second, (N_CTX, TOKENS_PER_SHARD), 0, 1024)
    limit = jnp.right_shift(jnp.full((N_CTX, 1), 256, jnp.int32), level)
    position = jnp.arange(PACKED_TOKENS, dtype=jnp.int32).reshape(N_CTX, TOKENS_PER_SHARD)
    local = jnp.arange(TOKENS_PER_SHARD, dtype=jnp.int32)[None, :]
    cut = (rolled < limit) | (local == 0) | (position == PACKED_TOKENS - 1)
    marks = jnp.where(cut, position, 0)
    return lax.cummax(marks, axis=1).reshape(PACKED_TOKENS).astype(jnp.int32)


def level_of(stream_key, extent, cuts, low, top_value):
    loudness = 1.0
    for dim, blocks in cuts:
        heights = jax.random.uniform(jax.random.fold_in(jax.random.fold_in(stream_key, 6), dim), (blocks,), jnp.float32, low / len(cuts), top_value / len(cuts))
        loudness = loudness * jnp.repeat(jnp.exp(heights), extent[dim] // blocks).reshape((-1,) + (1,) * (len(extent) - 1 - dim))
    return loudness


def noise(own_key, shape, deviation, bound, shards=(), kind=jnp.bfloat16):
    gain = level_of(own_key, shape, shards, -0.22, 0.18) if shards else 1.0
    array = jax.random.normal(own_key, shape, jnp.float32) * deviation * gain
    return jnp.minimum(jnp.maximum(array, -bound), bound).astype(kind)


def setup_inputs(seed: int = 0) -> dict:
    arg_keys = jax.random.split(jax.random.key(seed), 6)
    queries = draw_queries(jax.random.fold_in(arg_keys[5], 71), 0)
    keys = draw_keys(jax.random.fold_in(arg_keys[5], 71), 0)
    values = noise(arg_keys[2], (PACKED_TOKENS, KEY_VALUE_HEADS * HEAD_SIZE), 1.0, 6.0, ((0, 128), (1, 4)))
    output_gradient = noise(arg_keys[3], (PACKED_TOKENS, QUERY_HEADS * HEAD_SIZE), 1.0, 6.0, ((0, 128), (1, 4)))
    doc_start = draw_doc_start(jax.random.fold_in(arg_keys[5], 71), 0)
    return dict(queries=queries, keys=keys, values=values, output_gradient=output_gradient, doc_start=doc_start)


def shard_attention(items):
    q, k, v, grad, start = items
    rows = q.shape[0]
    scale = 1.0 / math.sqrt(HEAD_SIZE)
    place = jnp.arange(rows)
    visible = (start[:, None] == start[None, :]) & (place[None, :] <= place[:, None])
    qf = q.astype(jnp.float32)
    kf = k.astype(jnp.float32)
    vf = v.astype(jnp.float32)
    gf = grad.astype(jnp.float32)
    score = jnp.einsum('qhgd,khd->hgqk', qf, kf) * scale
    score = jnp.where(visible[None, None], score, -1e+30)
    top = lax.optimization_barrier(jnp.max(score, axis=-1, keepdims=True))
    expo = jnp.where(visible[None, None], jnp.exp(score - top), 0.0)
    prob = expo / lax.optimization_barrier(jnp.sum(expo, axis=-1, keepdims=True))
    prob_b = lax.optimization_barrier(prob.astype(jnp.bfloat16))
    attended = jnp.einsum('hgqk,khd->qhgd', prob_b.astype(jnp.float32), vf).astype(jnp.bfloat16)
    attended = lax.optimization_barrier(attended)
    delta = lax.optimization_barrier(jnp.sum(gf * attended.astype(jnp.float32), axis=-1)).transpose(1, 2, 0)
    dprob = jnp.einsum('qhgd,khd->hgqk', gf, vf)
    dscore = (prob * (dprob - delta[..., None]) * scale).astype(jnp.bfloat16)
    dscore = lax.optimization_barrier(dscore).astype(jnp.float32)
    query_gradient = jnp.einsum('hgqk,khd->qhgd', dscore, kf).astype(jnp.bfloat16)
    key_gradient = jnp.einsum('hgqk,qhgd->khd', dscore, qf).astype(jnp.bfloat16)
    value_gradient = jnp.einsum('hgqk,qhgd->khd', prob_b.astype(jnp.float32), gf).astype(jnp.bfloat16)
    return (attended, query_gradient, key_gradient, value_gradient)

def reference(queries, keys, values, output_gradient, doc_start):
    group_width = QUERY_HEADS // KEY_VALUE_HEADS
    queries_five_axis = queries.reshape(N_CTX, TOKENS_PER_SHARD, KEY_VALUE_HEADS, group_width, HEAD_SIZE)
    keys_four_axis = keys.reshape(N_CTX, TOKENS_PER_SHARD, KEY_VALUE_HEADS, HEAD_SIZE)
    values_four_axis = values.reshape(N_CTX, TOKENS_PER_SHARD, KEY_VALUE_HEADS, HEAD_SIZE)
    gradient_five_axis = output_gradient.reshape(N_CTX, TOKENS_PER_SHARD, KEY_VALUE_HEADS, group_width, HEAD_SIZE)
    s2 = doc_start.reshape(N_CTX, TOKENS_PER_SHARD)
    attended, query_gradient, key_gradient, value_gradient = lax.map(shard_attention, (queries_five_axis, keys_four_axis, values_four_axis, gradient_five_axis, s2))
    return (attended.reshape(PACKED_TOKENS, QUERY_HEADS * HEAD_SIZE), query_gradient.reshape(PACKED_TOKENS, QUERY_HEADS * HEAD_SIZE), key_gradient.reshape(PACKED_TOKENS, KEY_VALUE_HEADS * HEAD_SIZE), value_gradient.reshape(PACKED_TOKENS, KEY_VALUE_HEADS * HEAD_SIZE))
```

```python
import functools
import math

import jax
import jax.numpy as jnp
from jax import lax
from jax.experimental import pallas as pl
from jax.experimental.pallas import tpu as pltpu
from jax.sharding import PartitionSpec as P

MESH = pl.DeviceIdType.MESH
BF, F32 = jnp.bfloat16, jnp.float32
NT = (((1,), (1,)), ((), ()))
NN = (((1,), (0,)), ((), ()))
HEAD = 128
TILE = 128
HEADS = 8
ROWS = 512
BLOCKS = 4
SCALE = 1.0 / math.sqrt(HEAD)
SCALE2 = math.log2(math.e) / math.sqrt(HEAD)
FIRST = (0, 128, 384, 768)
STACKED = 1280
ORDER = (2, 1, 3, 0)
BARRIER_AFTER = 1
WIDTH = 4
PIECES = 1
VM2 = 2**20
GROUPS = HEADS // WIDTH


def head_cols(first, count=1):
    return pl.ds(pl.multiple_of(first * HEAD, HEAD), count * HEAD)


def stacked(ref, t, p):
    rows = slice(TILE * t, TILE * (t + 1))
    return [ref[rows, head_cols(p * WIDTH + x)] for x in range(WIDTH)]


def prepare(t, base, start, k, kaug):
    n, o = TILE * (t + 1), FIRST[t]
    kaug[o : o + n, 0:HEAD] = k[0:n, :]
    first = (start[pl.ds(TILE * t, TILE)] - base)[None, :]
    j = lax.broadcasted_iota(jnp.int32, (n, TILE), 0)
    i = lax.broadcasted_iota(jnp.int32, (n, TILE), 1) + TILE * t
    kaug[o : o + n, HEAD : 2 * HEAD] = jnp.where((j >= first) & (j <= i), 0.0, -1e30).astype(BF)


def forward(t, p, q, kaug, vt, prob, out):
    n, o = TILE * (t + 1), FIRST[t]
    eye = lax.broadcasted_iota(jnp.int32, (TILE, TILE), 0) == lax.broadcasted_iota(
        jnp.int32, (TILE, TILE), 1
    )
    eye = eye.astype(F32).astype(BF)
    queries = jnp.concatenate([jnp.concatenate([x, eye], 1) for x in stacked(q, t, p)], 0)
    score = lax.dot_general(kaug[o : o + n, :], queries, NT, preferred_element_type=F32)
    top = jnp.max(score, axis=0, keepdims=True)
    expo = jnp.exp2((score - top) * SCALE2)
    prob_b = (expo * (1.0 / jnp.sum(expo, axis=0, keepdims=True))).astype(BF)
    prob[p, o : o + n, :] = prob_b
    out_t = lax.dot_general(vt[:, 0:n], prob_b, NN, preferred_element_type=F32)
    for x in range(WIDTH):
        out[TILE * t : TILE * (t + 1), head_cols(p * WIDTH + x)] = out_t[
            :, HEAD * x : HEAD * (x + 1)
        ].T.astype(BF)


def backward(t, p, q, g, v, kt, prob, dq, dk, dv):
    n, o = TILE * (t + 1), FIRST[t]
    queries = jnp.concatenate(stacked(q, t, p), 0)
    grads = jnp.concatenate(stacked(g, t, p), 0)
    prob_b = prob[p, o : o + n, :]
    dprob = lax.dot_general(v[0:n, :], grads, NT, preferred_element_type=F32)
    prob_f = prob_b.astype(F32)
    delta = jnp.sum(prob_f * dprob, axis=0, keepdims=True)
    dscore = (prob_f * (dprob - delta)).astype(BF)
    dq_t = lax.dot_general(kt[:, 0:n], dscore, NN, preferred_element_type=F32) * SCALE
    for x in range(WIDTH):
        dq[TILE * t : TILE * (t + 1), head_cols(p * WIDTH + x)] = dq_t[
            :, HEAD * x : HEAD * (x + 1)
        ].T.astype(BF)
    dk[0:n, :] += lax.dot_general(dscore, queries, NN, preferred_element_type=F32)
    dv[0:n, :] += lax.dot_general(prob_b, grads, NN, preferred_element_type=F32)


def groups(body):
    def step(p, carry):
        body(p)
        return carry

    lax.fori_loop(0, GROUPS, step, 0)


def kernel(
    q_in, k_in, v_in, g_in, start_in,
    att_out, dq_out, dk_out, dv_out,
    q, k, v, g, start, kaug, kt, vt, prob, out, dq, dk, dv, dk_b, dv_b,
    q_sem, g_sem, kv_sem, send_sem, recv_sem, own_sem, dq_sem, kv_out_sem,
):
    me = lax.axis_index("tp")
    base = lax.axis_index("ctx") * ROWS
    peers = [lax.rem(me + off, BLOCKS) for off in ORDER]
    barrier = pltpu.get_barrier_semaphore()
    for peer in peers[:3]:
        pl.semaphore_signal(barrier, inc=1, device_id={"tp": peer}, device_id_type=MESH)

    loads = [
        pltpu.make_async_copy(src, dst, kv_sem.at[i])
        for i, (src, dst) in enumerate(((k_in, k), (start_in, start), (v_in, v)))
    ]
    for copy in loads:
        copy.start()

    def block(ref, t):
        return ref.at[pl.ds(pl.multiple_of(t * TILE, TILE), TILE)]

    def load(src, dst, sems):
        copies = []
        for i, peer in enumerate(peers):
            copies.append(pltpu.make_async_copy(block(src, peer), block(dst, peer), sems.at[i]))
            copies[-1].start()
        return copies

    q_loads = load(q_in, q, q_sem)
    g_loads = load(g_in, g, g_sem)
    for copy in loads:
        copy.wait()
    vt[...] = v[...].T

    mine = pl.ds(pl.multiple_of(me * HEADS * HEAD, HEADS * HEAD), HEADS * HEAD)
    sends = []

    def send(i):
        sends.append(
            pltpu.make_async_remote_copy(
                src_ref=block(out, peers[i]),
                dst_ref=att_out.at[:, mine],
                send_sem=send_sem.at[i],
                recv_sem=recv_sem.at[i],
                device_id={"tp": peers[i]},
                device_id_type=MESH,
            )
        )
        sends[-1].start()

    for i, peer in enumerate(peers):
        q_loads[i].wait()

        def one(t):
            prepare(t, base, start, k, kaug)
            groups(lambda p: forward(t, p, q, kaug, vt, prob, out))

        lax.switch(peer, [functools.partial(one, t) for t in range(BLOCKS)])
        if i == BARRIER_AFTER:
            pl.semaphore_wait(barrier, 3)
            for early in range(i + 1):
                send(early)
        elif i > BARRIER_AFTER and i < 3:
            send(i)
    own = pltpu.make_async_copy(block(out, me), att_out.at[:, mine], own_sem)
    own.start()

    kt[...] = k[...].T
    dk[...] = jnp.zeros_like(dk)
    dv[...] = jnp.zeros_like(dv)
    for copy in g_loads:
        copy.wait()
    stores = []
    for t in range(BLOCKS):
        groups(lambda p, t=t: backward(t, p, q, g, v, kt, prob, dq, dk, dv))
        stores.append(
            pltpu.make_async_copy(
                dq.at[pl.ds(TILE * t, TILE)], dq_out.at[pl.ds(TILE * t, TILE)], dq_sem.at[t]
            )
        )
        stores[-1].start()
    dk_b[...] = (dk[...] * SCALE).astype(BF)
    dv_b[...] = dv[...].astype(BF)
    for i, (src, dst) in enumerate(((dk_b, dk_out), (dv_b, dv_out))):
        stores.append(pltpu.make_async_copy(src, dst, kv_out_sem.at[i]))
        stores[-1].start()
    for copy in stores:
        copy.wait()
    own.wait()
    for copy in sends:
        copy.wait()


def deliver(*refs):
    sems = refs[8]
    copies = []
    for i in range(4):
        rows = refs[i].shape[0]
        pieces = PIECES if i < 2 else 1
        for c in range(pieces):
            part = pl.ds(c * (rows // pieces), rows // pieces)
            copies.append(
                pltpu.make_async_copy(refs[i].at[part], refs[4 + i].at[part], sems.at[i, c])
            )
            copies[-1].start()
    for copy in copies:
        copy.wait()


def on_device(queries, keys, values, output_gradient, doc_start):
    anywhere = pl.BlockSpec(memory_space=pl.ANY)
    hbm = pl.BlockSpec(memory_space=pltpu.HBM)
    dma = pltpu.SemaphoreType.DMA
    queries, keys, values, output_gradient, doc_start = (
        pltpu.with_memory_space_constraint(x, pltpu.HBM)
        for x in (queries, keys, values, output_gradient, doc_start)
    )
    results = pl.pallas_call(
        kernel,
        out_shape=(
            jax.ShapeDtypeStruct((TILE, BLOCKS * HEADS * HEAD), BF),
            jax.ShapeDtypeStruct((ROWS, HEADS * HEAD), BF),
            jax.ShapeDtypeStruct((ROWS, HEAD), BF),
            jax.ShapeDtypeStruct((ROWS, HEAD), BF),
        ),
        in_specs=[hbm] * 5,
        out_specs=(anywhere,) * 4,
        scratch_shapes=[
            pltpu.VMEM((ROWS, HEADS * HEAD), BF),
            pltpu.VMEM((ROWS, HEAD), BF),
            pltpu.VMEM((ROWS, HEAD), BF),
            pltpu.VMEM((ROWS, HEADS * HEAD), BF),
            pltpu.VMEM((ROWS,), jnp.int32),
            pltpu.VMEM((STACKED, 2 * HEAD), BF),
            pltpu.VMEM((HEAD, ROWS), BF),
            pltpu.VMEM((HEAD, ROWS), BF),
            pltpu.VMEM((GROUPS, STACKED, WIDTH * TILE), BF),
            pltpu.VMEM((ROWS, HEADS * HEAD), BF),
            pltpu.VMEM((ROWS, HEADS * HEAD), BF),
            pltpu.VMEM((ROWS, HEAD), F32),
            pltpu.VMEM((ROWS, HEAD), F32),
            pltpu.VMEM((ROWS, HEAD), BF),
            pltpu.VMEM((ROWS, HEAD), BF),
            dma((BLOCKS,)),
            dma((BLOCKS,)),
            dma((3,)),
            dma((3,)),
            dma((3,)),
            dma,
            dma((BLOCKS,)),
            dma((2,)),
        ],
        compiler_params=pltpu.CompilerParams(
            collective_id=0, has_side_effects=True, vmem_limit_bytes=48 * 2**20
        ),
    )(queries, keys, values, output_gradient, doc_start)
    return pl.pallas_call(
        deliver,
        out_shape=tuple(jax.ShapeDtypeStruct(x.shape, x.dtype) for x in results),
        in_specs=[anywhere] * 4,
        out_specs=(hbm,) * 4,
        scratch_shapes=[dma((4, PIECES))],
        compiler_params=pltpu.CompilerParams(vmem_limit_bytes=VM2),
    )(*results)


def solution(mesh):
    return jax.shard_map(
        on_device,
        mesh=mesh,
        in_specs=(P("ctx", "tp"), P("ctx", "tp"), P("ctx", "tp"), P("ctx", "tp"), P("ctx")),
        out_specs=(P(("ctx", "tp"), None), P("ctx", "tp"), P("ctx", "tp"), P("ctx", "tp")),
        check_vma=False,
    )
```

```python
import functools
import math

import jax
import jax.numpy as jnp
from jax import lax
from jax.experimental import pallas as pl
from jax.experimental.pallas import tpu as pltpu
from jax.sharding import PartitionSpec as P

MESH = pl.DeviceIdType.MESH
BF, F32 = jnp.bfloat16, jnp.float32
NT = (((1,), (1,)), ((), ()))
NN = (((1,), (0,)), ((), ()))
HEAD = 128
TILE = 128
HEADS = 8
ROWS = 512
BLOCKS = 4
SCALE = 1.0 / math.sqrt(HEAD)
SCALE2 = math.log2(math.e) / math.sqrt(HEAD)
FIRST = (0, 128, 384, 768)
STACKED = 1280
ORDER = (2, 1, 3, 0)
PART = 4
PARTS = HEADS // PART


def head_cols(first, count=1):
    return pl.ds(pl.multiple_of(first * HEAD, HEAD), count * HEAD)


def stacked(ref, t, first, count):
    rows = slice(TILE * t, TILE * (t + 1))
    return [ref[rows, head_cols(first + x)] for x in range(count)]


def prepare(t, base, start, k, kaug):
    n, o = TILE * (t + 1), FIRST[t]
    kaug[o : o + n, 0:HEAD] = k[0:n, :]
    first = (start[pl.ds(TILE * t, TILE)] - base)[None, :]
    j = lax.broadcasted_iota(jnp.int32, (n, TILE), 0)
    i = lax.broadcasted_iota(jnp.int32, (n, TILE), 1) + TILE * t
    kaug[o : o + n, HEAD : 2 * HEAD] = jnp.where((j >= first) & (j <= i), 0.0, -1e30).astype(BF)


def forward(t, first, count, q, kaug, vt, prob, out):
    n, o = TILE * (t + 1), FIRST[t]
    eye = lax.broadcasted_iota(jnp.int32, (TILE, TILE), 0) == lax.broadcasted_iota(
        jnp.int32, (TILE, TILE), 1
    )
    eye = eye.astype(F32).astype(BF)
    queries = [jnp.concatenate([x, eye], 1) for x in stacked(q, t, first, count)]
    queries = jnp.concatenate(queries, 0)
    score = lax.dot_general(kaug[o : o + n, :], queries, NT, preferred_element_type=F32)
    top = jnp.max(score, axis=0, keepdims=True)
    expo = jnp.exp2((score - top) * SCALE2)
    prob_b = (expo * (1.0 / jnp.sum(expo, axis=0, keepdims=True))).astype(BF)
    prob[o : o + n, head_cols(first, count)] = prob_b
    out_t = lax.dot_general(vt[:, 0:n], prob_b, NN, preferred_element_type=F32)
    for x in range(count):
        out[TILE * t : TILE * (t + 1), head_cols(first + x)] = out_t[
            :, HEAD * x : HEAD * (x + 1)
        ].T.astype(BF)


def backward(t, q, g, v, kt, prob, dq, dk, dv):
    n, o = TILE * (t + 1), FIRST[t]
    queries = jnp.concatenate(stacked(q, t, 0, HEADS), 0)
    grads = jnp.concatenate(stacked(g, t, 0, HEADS), 0)
    prob_b = prob[o : o + n, :]
    dprob = lax.dot_general(v[0:n, :], grads, NT, preferred_element_type=F32)
    prob_f = prob_b.astype(F32)
    delta = jnp.sum(prob_f * dprob, axis=0, keepdims=True)
    dscore = (prob_f * (dprob - delta)).astype(BF)
    dq_t = lax.dot_general(kt[:, 0:n], dscore, NN, preferred_element_type=F32) * SCALE
    for x in range(HEADS):
        dq[TILE * t : TILE * (t + 1), head_cols(x)] = dq_t[:, HEAD * x : HEAD * (x + 1)].T.astype(
            BF
        )
    dk[0:n, :] += lax.dot_general(dscore, queries, NN, preferred_element_type=F32)
    dv[0:n, :] += lax.dot_general(prob_b, grads, NN, preferred_element_type=F32)


def kernel(
    q_in, k_in, v_in, g_in, start_in,
    att_out, dq_out, dk_out, dv_out,
    q, k, v, g, start, kaug, kt, vt, prob, out, dq, dk, dv, dk_b, dv_b,
    q_sem, g_sem, kv_sem, send_sem, recv_sem, own_sem, dq_sem, kv_out_sem,
):
    me = lax.axis_index("tp")
    base = lax.axis_index("ctx") * ROWS
    peers = [lax.rem(me + off, BLOCKS) for off in ORDER]

    def block(ref, t):
        return ref.at[pl.ds(pl.multiple_of(t * TILE, TILE), TILE)]

    def load(src, dst, sem):
        copy = pltpu.make_async_copy(src, dst, sem)
        copy.start()
        return copy

    k_load = load(k_in, k, kv_sem.at[0])
    q_loads = [load(block(q_in, peers[0]), block(q, peers[0]), q_sem.at[0])]
    start_load = load(start_in, start, kv_sem.at[1])
    v_load = load(v_in, v, kv_sem.at[2])
    barrier = pltpu.get_barrier_semaphore()
    for peer in peers[:3]:
        pl.semaphore_signal(barrier, inc=1, device_id={"tp": peer}, device_id_type=MESH)
    for i in range(1, BLOCKS):
        q_loads.append(load(block(q_in, peers[i]), block(q, peers[i]), q_sem.at[i]))
    mine = me * HEADS

    def send(i, first, count, slot):
        copy = pltpu.make_async_remote_copy(
            src_ref=block(out, peers[i]).at[:, head_cols(first, count)],
            dst_ref=att_out.at[:, head_cols(mine + first, count)],
            send_sem=send_sem.at[slot],
            recv_sem=recv_sem.at[slot],
            device_id={"tp": peers[i]},
            device_id_type=MESH,
        )
        copy.start()
        return copy

    def branch(i, body):
        lax.switch(peers[i], [functools.partial(body, t) for t in range(BLOCKS)])

    start_load.wait()
    k_load.wait()
    q_loads[0].wait()
    branch(0, lambda t: prepare(t, base, start, k, kaug))
    v_load.wait()
    vt[...] = v[...].T
    sends = []
    for part in range(PARTS):
        branch(0, lambda t: forward(t, part * PART, PART, q, kaug, vt, prob, out))
        if part == 0:
            pl.semaphore_wait(barrier, 3)
        sends.append(send(0, part * PART, PART, part))
    g_loads = [load(block(g_in, t), block(g, t), g_sem.at[t]) for t in range(BLOCKS)]

    def whole(t):
        prepare(t, base, start, k, kaug)
        forward(t, 0, HEADS, q, kaug, vt, prob, out)

    for i in range(1, BLOCKS):
        q_loads[i].wait()
        branch(i, whole)
        if i < 3:
            sends.append(send(i, 0, HEADS, PARTS + i - 1))
    own = pltpu.make_async_copy(block(out, me), att_out.at[:, head_cols(mine, HEADS)], own_sem)
    own.start()

    kt[...] = k[...].T
    dk[...] = jnp.zeros_like(dk)
    dv[...] = jnp.zeros_like(dv)
    for copy in g_loads:
        copy.wait()
    stores = []
    for t in range(BLOCKS):
        backward(t, q, g, v, kt, prob, dq, dk, dv)
        stores.append(
            pltpu.make_async_copy(
                dq.at[pl.ds(TILE * t, TILE)], dq_out.at[pl.ds(TILE * t, TILE)], dq_sem.at[t]
            )
        )
        stores[-1].start()
    dk_b[...] = (dk[...] * SCALE).astype(BF)
    dv_b[...] = dv[...].astype(BF)
    for i, (src, dst) in enumerate(((dk_b, dk_out), (dv_b, dv_out))):
        stores.append(pltpu.make_async_copy(src, dst, kv_out_sem.at[i]))
        stores[-1].start()
    for copy in stores:
        copy.wait()
    own.wait()
    for copy in sends:
        copy.wait()


def deliver(*refs):
    sems = refs[8]
    copies = [pltpu.make_async_copy(refs[i], refs[4 + i], sems.at[i]) for i in range(4)]
    for copy in copies:
        copy.start()
    for copy in copies:
        copy.wait()


def on_device(queries, keys, values, output_gradient, doc_start):
    anywhere = pl.BlockSpec(memory_space=pl.ANY)
    hbm = pl.BlockSpec(memory_space=pltpu.HBM)
    dma = pltpu.SemaphoreType.DMA
    queries, keys, values, output_gradient, doc_start = (
        pltpu.with_memory_space_constraint(x, pltpu.HBM)
        for x in (queries, keys, values, output_gradient, doc_start)
    )
    results = pl.pallas_call(
        kernel,
        out_shape=(
            jax.ShapeDtypeStruct((TILE, BLOCKS * HEADS * HEAD), BF),
            jax.ShapeDtypeStruct((ROWS, HEADS * HEAD), BF),
            jax.ShapeDtypeStruct((ROWS, HEAD), BF),
            jax.ShapeDtypeStruct((ROWS, HEAD), BF),
        ),
        in_specs=[hbm] * 5,
        out_specs=(anywhere,) * 4,
        scratch_shapes=[
            pltpu.VMEM((ROWS, HEADS * HEAD), BF),
            pltpu.VMEM((ROWS, HEAD), BF),
            pltpu.VMEM((ROWS, HEAD), BF),
            pltpu.VMEM((ROWS, HEADS * HEAD), BF),
            pltpu.VMEM((ROWS,), jnp.int32),
            pltpu.VMEM((STACKED, 2 * HEAD), BF),
            pltpu.VMEM((HEAD, ROWS), BF),
            pltpu.VMEM((HEAD, ROWS), BF),
            pltpu.VMEM((STACKED, HEADS * TILE), BF),
            pltpu.VMEM((ROWS, HEADS * HEAD), BF),
            pltpu.VMEM((ROWS, HEADS * HEAD), BF),
            pltpu.VMEM((ROWS, HEAD), F32),
            pltpu.VMEM((ROWS, HEAD), F32),
            pltpu.VMEM((ROWS, HEAD), BF),
            pltpu.VMEM((ROWS, HEAD), BF),
            dma((BLOCKS,)),
            dma((BLOCKS,)),
            dma((3,)),
            dma((PARTS + 2,)),
            dma((PARTS + 2,)),
            dma,
            dma((BLOCKS,)),
            dma((2,)),
        ],
        compiler_params=pltpu.CompilerParams(
            collective_id=0, has_side_effects=True, vmem_limit_bytes=48 * 2**20
        ),
    )(queries, keys, values, output_gradient, doc_start)
    return pl.pallas_call(
        deliver,
        out_shape=tuple(jax.ShapeDtypeStruct(x.shape, x.dtype) for x in results),
        in_specs=[anywhere] * 4,
        out_specs=(hbm,) * 4,
        scratch_shapes=[dma((4,))],
        compiler_params=pltpu.CompilerParams(vmem_limit_bytes=2**20),
    )(*results)


def solution(mesh):
    return jax.shard_map(
        on_device,
        mesh=mesh,
        in_specs=(P("ctx", "tp"), P("ctx", "tp"), P("ctx", "tp"), P("ctx", "tp"), P("ctx")),
        out_specs=(P(("ctx", "tp"), None), P("ctx", "tp"), P("ctx", "tp"), P("ctx", "tp")),
        check_vma=False,
    )
```

```python
import functools
import math

import jax
import jax.numpy as jnp
from jax import lax
from jax.experimental import pallas as pl
from jax.experimental.pallas import tpu as pltpu
from jax.sharding import PartitionSpec as P

MESH = pl.DeviceIdType.MESH
BF, F32 = jnp.bfloat16, jnp.float32
NT = (((1,), (1,)), ((), ()))
NN = (((1,), (0,)), ((), ()))
HEAD = 128
TILE = 128
HEADS = 8
ROWS = 512
BLOCKS = 4
SCALE = 1.0 / math.sqrt(HEAD)
SCALE2 = math.log2(math.e) / math.sqrt(HEAD)
FIRST = (0, 128, 384, 768)
STACKED = 1280
ORDER = (2, 1, 3, 0)
PART = 4
PARTS = HEADS // PART


def head_cols(first, count=1):
    return pl.ds(pl.multiple_of(first * HEAD, HEAD), count * HEAD)


def stacked(ref, t, first, count):
    rows = slice(TILE * t, TILE * (t + 1))
    return [ref[rows, head_cols(first + x)] for x in range(count)]


def make_masks(base, start, masks):
    for t in range(BLOCKS):
        n, o = TILE * (t + 1), FIRST[t]
        first = (start[pl.ds(TILE * t, TILE)] - base)[None, :]
        j = lax.broadcasted_iota(jnp.int32, (n, TILE), 0)
        i = lax.broadcasted_iota(jnp.int32, (n, TILE), 1) + TILE * t
        masks[o : o + n, :] = jnp.where((j >= first) & (j <= i), 0.0, -1e30)


def forward(t, first, count, q, k, masks, vt, prob, out):
    n, o = TILE * (t + 1), FIRST[t]
    queries = jnp.concatenate(stacked(q, t, first, count), 0)
    score = lax.dot_general(k[0:n, :], queries, NT, preferred_element_type=F32)
    score += jnp.concatenate([masks[o : o + n, :]] * count, 1)
    top = jnp.max(score, axis=0, keepdims=True)
    expo = jnp.exp2((score - top) * SCALE2)
    prob_b = (expo * (1.0 / jnp.sum(expo, axis=0, keepdims=True))).astype(BF)
    prob[o : o + n, head_cols(first, count)] = prob_b
    out_t = lax.dot_general(vt[:, 0:n], prob_b, NN, preferred_element_type=F32)
    for x in range(count):
        out[TILE * t : TILE * (t + 1), head_cols(first + x)] = out_t[
            :, HEAD * x : HEAD * (x + 1)
        ].T.astype(BF)


def backward(t, q, g, v, kt, prob, dq, dk, dv):
    n, o = TILE * (t + 1), FIRST[t]
    queries = jnp.concatenate(stacked(q, t, 0, HEADS), 0)
    grads = jnp.concatenate(stacked(g, t, 0, HEADS), 0)
    prob_b = prob[o : o + n, :]
    dprob = lax.dot_general(v[0:n, :], grads, NT, preferred_element_type=F32)
    prob_f = prob_b.astype(F32)
    delta = jnp.sum(prob_f * dprob, axis=0, keepdims=True)
    dscore = (prob_f * (dprob - delta)).astype(BF)
    dq_t = lax.dot_general(kt[:, 0:n], dscore, NN, preferred_element_type=F32) * SCALE
    for x in range(HEADS):
        dq[TILE * t : TILE * (t + 1), head_cols(x)] = dq_t[:, HEAD * x : HEAD * (x + 1)].T.astype(
            BF
        )
    dk[0:n, :] += lax.dot_general(dscore, queries, NN, preferred_element_type=F32)
    dv[0:n, :] += lax.dot_general(prob_b, grads, NN, preferred_element_type=F32)


def kernel(
    q_in, k_in, v_in, g_in, start_in,
    att_out, dq_out, dk_out, dv_out,
    q, k, v, g, start, masks, kt, vt, prob, out, dq, dk, dv, dk_b, dv_b,
    sems, send_sem, recv_sem,
):
    me = lax.axis_index("tp")
    base = lax.axis_index("ctx") * ROWS
    peers = [lax.rem(me + off, BLOCKS) for off in ORDER]

    def block(ref, t):
        return ref.at[pl.ds(pl.multiple_of(t * TILE, TILE), TILE)]

    def move(src, dst, sem):
        copy = pltpu.make_async_copy(src, dst, sem)
        copy.start()
        return copy

    k_load = move(k_in, k, sems.at[0])
    q_load = move(block(q_in, peers[0]), block(q, peers[0]), sems.at[1])
    start_load = move(start_in, start, sems.at[2])
    v_load = move(v_in, v, sems.at[3])
    barrier = pltpu.get_barrier_semaphore()
    for peer in peers[:3]:
        pl.semaphore_signal(barrier, inc=1, device_id={"tp": peer}, device_id_type=MESH)
    for i in range(1, BLOCKS):
        move(block(q_in, peers[i]), block(q, peers[i]), sems.at[4])
    mine = me * HEADS

    def send(i, first, count):
        pltpu.make_async_remote_copy(
            src_ref=block(out, peers[i]).at[:, head_cols(first, count)],
            dst_ref=att_out.at[:, head_cols(mine + first, count)],
            send_sem=send_sem,
            recv_sem=recv_sem,
            device_id={"tp": peers[i]},
            device_id_type=MESH,
        ).start()

    def arrived(ref, sem):
        pltpu.make_async_copy(ref, ref, sem).wait()

    def branch(i, body):
        lax.switch(peers[i], [functools.partial(body, t) for t in range(BLOCKS)])

    start_load.wait()
    make_masks(base, start, masks)
    k_load.wait()
    q_load.wait()
    v_load.wait()

    def partial(part, t):
        if part == 0:
            vt[...] = v[...].T
        forward(t, part * PART, PART, q, k, masks, vt, prob, out)

    for part in range(PARTS):
        branch(0, functools.partial(partial, part))
        if part == 0:
            pl.semaphore_wait(barrier, 3)
        send(0, part * PART, PART)
    g_load = move(g_in, g, sems.at[5])

    def whole(t):
        forward(t, 0, HEADS, q, k, masks, vt, prob, out)

    others = pl.ds(0, (BLOCKS - 1) * TILE)
    arrived(q.at[others], sems.at[4])
    for i in range(1, BLOCKS):
        branch(i, whole)
        if i < 3:
            send(i, 0, HEADS)
    own = move(block(out, me), att_out.at[:, head_cols(mine, HEADS)], sems.at[1])

    kt[...] = k[...].T
    dk[...] = jnp.zeros_like(dk)
    dv[...] = jnp.zeros_like(dv)
    g_load.wait()
    for t in range(BLOCKS):
        backward(t, q, g, v, kt, prob, dq, dk, dv)
    dk_b[...] = (dk[...] * SCALE).astype(BF)
    dv_b[...] = dv[...].astype(BF)
    stores = [
        move(dq, dq_out, sems.at[0]),
        move(dk_b, dk_out, sems.at[2]),
        move(dv_b, dv_out, sems.at[3]),
        own,
    ]
    for copy in stores:
        copy.wait()
    arrived(out.at[others], send_sem)
    arrived(att_out.at[:, head_cols(0, (BLOCKS - 1) * HEADS)], recv_sem)


def deliver(*refs):
    sems = refs[8]
    copies = [pltpu.make_async_copy(refs[i], refs[4 + i], sems.at[i]) for i in range(4)]
    for copy in copies:
        copy.start()
    for copy in copies:
        copy.wait()


def on_device(queries, keys, values, output_gradient, doc_start):
    anywhere = pl.BlockSpec(memory_space=pl.ANY)
    hbm = pl.BlockSpec(memory_space=pltpu.HBM)
    dma = pltpu.SemaphoreType.DMA
    queries, keys, values, output_gradient, doc_start = (
        pltpu.with_memory_space_constraint(x, pltpu.HBM)
        for x in (queries, keys, values, output_gradient, doc_start)
    )
    results = pl.pallas_call(
        kernel,
        out_shape=(
            jax.ShapeDtypeStruct((TILE, BLOCKS * HEADS * HEAD), BF),
            jax.ShapeDtypeStruct((ROWS, HEADS * HEAD), BF),
            jax.ShapeDtypeStruct((ROWS, HEAD), BF),
            jax.ShapeDtypeStruct((ROWS, HEAD), BF),
        ),
        in_specs=[hbm] * 5,
        out_specs=(anywhere,) * 4,
        scratch_shapes=[
            pltpu.VMEM((ROWS, HEADS * HEAD), BF),
            pltpu.VMEM((ROWS, HEAD), BF),
            pltpu.VMEM((ROWS, HEAD), BF),
            pltpu.VMEM((ROWS, HEADS * HEAD), BF),
            pltpu.VMEM((ROWS,), jnp.int32),
            pltpu.VMEM((STACKED, TILE), F32),
            pltpu.VMEM((HEAD, ROWS), BF),
            pltpu.VMEM((HEAD, ROWS), BF),
            pltpu.VMEM((STACKED, HEADS * TILE), BF),
            pltpu.VMEM((ROWS, HEADS * HEAD), BF),
            pltpu.VMEM((ROWS, HEADS * HEAD), BF),
            pltpu.VMEM((ROWS, HEAD), F32),
            pltpu.VMEM((ROWS, HEAD), F32),
            pltpu.VMEM((ROWS, HEAD), BF),
            pltpu.VMEM((ROWS, HEAD), BF),
            dma((6,)),
            dma,
            dma,
        ],
        compiler_params=pltpu.CompilerParams(
            collective_id=0, has_side_effects=True, vmem_limit_bytes=48 * 2**20
        ),
    )(queries, keys, values, output_gradient, doc_start)
    return pl.pallas_call(
        deliver,
        out_shape=tuple(jax.ShapeDtypeStruct(x.shape, x.dtype) for x in results),
        in_specs=[anywhere] * 4,
        out_specs=(hbm,) * 4,
        scratch_shapes=[dma((4,))],
        compiler_params=pltpu.CompilerParams(vmem_limit_bytes=2**20),
    )(*results)


def solution(mesh):
    return jax.shard_map(
        on_device,
        mesh=mesh,
        in_specs=(P("ctx", "tp"), P("ctx", "tp"), P("ctx", "tp"), P("ctx", "tp"), P("ctx")),
        out_specs=(P(("ctx", "tp"), None), P("ctx", "tp"), P("ctx", "tp"), P("ctx", "tp")),
        check_vma=False,
    )
```

```python
import functools
import math

import jax
import jax.numpy as jnp
from jax import lax
from jax.experimental import pallas as pl
from jax.experimental.pallas import tpu as pltpu
from jax.sharding import PartitionSpec as P

MESH = pl.DeviceIdType.MESH
BF, F32 = jnp.bfloat16, jnp.float32
NT = (((1,), (1,)), ((), ()))
NN = (((1,), (0,)), ((), ()))
HEAD = 128
TILE = 128
HEADS = 8
ROWS = 512
BLOCKS = 4
SCALE = 1.0 / math.sqrt(HEAD)
SCALE2 = math.log2(math.e) / math.sqrt(HEAD)
FIRST = (0, 128, 384, 768)
STACKED = 1280
ORDER = (2, 1, 3, 0)
PART = 4
PARTS = HEADS // PART


def head_cols(first, count=1):
    return pl.ds(pl.multiple_of(first * HEAD, HEAD), count * HEAD)


def stacked(ref, t, first, count):
    rows = slice(TILE * t, TILE * (t + 1))
    return [ref[rows, head_cols(first + x)] for x in range(count)]


def make_masks(base, start, masks):
    for t in range(BLOCKS):
        n, o = TILE * (t + 1), FIRST[t]
        first = (start[pl.ds(TILE * t, TILE)] - base)[None, :]
        j = lax.broadcasted_iota(jnp.int32, (n, TILE), 0)
        i = lax.broadcasted_iota(jnp.int32, (n, TILE), 1) + TILE * t
        masks[o : o + n, :] = jnp.where((j >= first) & (j <= i), 0.0, -1e30)


def forward(t, first, count, q, k, masks, vt, prob, out):
    n, o = TILE * (t + 1), FIRST[t]
    queries = jnp.concatenate(stacked(q, t, first, count), 0)
    score = lax.dot_general(k[0:n, :], queries, NT, preferred_element_type=F32)
    score += jnp.concatenate([masks[o : o + n, :]] * count, 1)
    top = jnp.max(score, axis=0, keepdims=True)
    expo = jnp.exp2((score - top) * SCALE2)
    out_t = lax.dot_general(vt[:, 0:n], expo.astype(BF), NN, preferred_element_type=F32)
    share = 1.0 / jnp.sum(expo, axis=0, keepdims=True)
    out_t = out_t * share
    prob[o : o + n, head_cols(first, count)] = (expo * share).astype(BF)
    for x in range(count):
        out[TILE * t : TILE * (t + 1), head_cols(first + x)] = out_t[
            :, HEAD * x : HEAD * (x + 1)
        ].T.astype(BF)


def backward(t, q, g, v, kt, prob, dq, dk, dv):
    n, o = TILE * (t + 1), FIRST[t]
    queries = jnp.concatenate(stacked(q, t, 0, HEADS), 0)
    grads = jnp.concatenate(stacked(g, t, 0, HEADS), 0)
    prob_b = prob[o : o + n, :]
    dprob = lax.dot_general(v[0:n, :], grads, NT, preferred_element_type=F32)
    prob_f = prob_b.astype(F32)
    delta = jnp.sum(prob_f * dprob, axis=0, keepdims=True)
    dscore = (prob_f * (dprob - delta)).astype(BF)
    dq_t = lax.dot_general(kt[:, 0:n], dscore, NN, preferred_element_type=F32) * SCALE
    for x in range(HEADS):
        dq[TILE * t : TILE * (t + 1), head_cols(x)] = dq_t[:, HEAD * x : HEAD * (x + 1)].T.astype(
            BF
        )
    dk[0:n, :] += lax.dot_general(dscore, queries, NN, preferred_element_type=F32)
    dv[0:n, :] += lax.dot_general(prob_b, grads, NN, preferred_element_type=F32)


def kernel(
    q_in, k_in, v_in, g_in, start_in,
    att_out, dq_out, dk_out, dv_out,
    q, k, v, g, start, masks, kt, vt, prob, out, dq, dk, dv, dk_b, dv_b,
    sems, send_sem, recv_sem,
):
    me = lax.axis_index("tp")
    base = lax.axis_index("ctx") * ROWS
    peers = [lax.rem(me + off, BLOCKS) for off in ORDER]

    def block(ref, t):
        return ref.at[pl.ds(pl.multiple_of(t * TILE, TILE), TILE)]

    def move(src, dst, sem):
        copy = pltpu.make_async_copy(src, dst, sem)
        copy.start()
        return copy

    for t in range(BLOCKS):
        move(block(k_in, t), block(k, t), sems.at[0])
    for x in range(HEADS):
        move(
            block(q_in, peers[0]).at[:, head_cols(x)],
            block(q, peers[0]).at[:, head_cols(x)],
            sems.at[0],
        )
    start_load = move(start_in, start, sems.at[1])
    for t in range(BLOCKS):
        move(block(v_in, t), block(v, t), sems.at[0])
    barrier = pltpu.get_barrier_semaphore()
    for peer in peers[:3]:
        pl.semaphore_signal(barrier, inc=1, device_id={"tp": peer}, device_id_type=MESH)
    for i in range(1, BLOCKS):
        move(block(q_in, peers[i]), block(q, peers[i]), sems.at[2])
    mine = me * HEADS

    def send(i, first, count):
        pltpu.make_async_remote_copy(
            src_ref=block(out, peers[i]).at[:, head_cols(first, count)],
            dst_ref=att_out.at[:, head_cols(mine + first, count)],
            send_sem=send_sem,
            recv_sem=recv_sem,
            device_id={"tp": peers[i]},
            device_id_type=MESH,
        ).start()

    def arrived(ref, sem):
        pltpu.make_async_copy(ref, ref, sem).wait()

    def branch(i, body):
        lax.switch(peers[i], [functools.partial(body, t) for t in range(BLOCKS)])

    start_load.wait()
    make_masks(base, start, masks)
    arrived(q.at[pl.ds(0, 2 * TILE)], sems.at[0])

    def partial(part, t):
        if part == 0:
            vt[...] = v[...].T
        forward(t, part * PART, PART, q, k, masks, vt, prob, out)

    for part in range(PARTS):
        branch(0, functools.partial(partial, part))
        if part == 0:
            pl.semaphore_wait(barrier, 3)
        send(0, part * PART, PART)
    g_load = move(g_in, g, sems.at[3])

    def whole(t):
        forward(t, 0, HEADS, q, k, masks, vt, prob, out)

    others = pl.ds(0, (BLOCKS - 1) * TILE)
    arrived(q.at[others], sems.at[2])
    for i in range(1, BLOCKS):
        branch(i, whole)
        if i < 3:
            send(i, 0, HEADS)
    move(block(out, me), att_out.at[:, head_cols(mine, HEADS)], sems.at[0])

    kt[...] = k[...].T
    dk[...] = jnp.zeros_like(dk)
    dv[...] = jnp.zeros_like(dv)
    g_load.wait()
    for t in range(BLOCKS):
        backward(t, q, g, v, kt, prob, dq, dk, dv)
    dk_b[...] = (dk[...] * SCALE).astype(BF)
    dv_b[...] = dv[...].astype(BF)
    move(dq, dq_out, sems.at[0])
    move(dk_b, dk_out, sems.at[0])
    move(dv_b, dv_out, sems.at[0])
    arrived(prob.at[pl.ds(0, 6 * TILE)], sems.at[0])
    arrived(out.at[others], send_sem)
    arrived(att_out.at[:, head_cols(0, (BLOCKS - 1) * HEADS)], recv_sem)


def deliver(*refs):
    sems = refs[8]
    copies = [pltpu.make_async_copy(refs[i], refs[4 + i], sems.at[i]) for i in range(4)]
    for copy in copies:
        copy.start()
    for copy in copies:
        copy.wait()


def on_device(queries, keys, values, output_gradient, doc_start):
    anywhere = pl.BlockSpec(memory_space=pl.ANY)
    hbm = pl.BlockSpec(memory_space=pltpu.HBM)
    dma = pltpu.SemaphoreType.DMA
    queries, keys, values, output_gradient, doc_start = (
        pltpu.with_memory_space_constraint(x, pltpu.HBM)
        for x in (queries, keys, values, output_gradient, doc_start)
    )
    results = pl.pallas_call(
        kernel,
        out_shape=(
            jax.ShapeDtypeStruct((TILE, BLOCKS * HEADS * HEAD), BF),
            jax.ShapeDtypeStruct((ROWS, HEADS * HEAD), BF),
            jax.ShapeDtypeStruct((ROWS, HEAD), BF),
            jax.ShapeDtypeStruct((ROWS, HEAD), BF),
        ),
        in_specs=[hbm] * 5,
        out_specs=(anywhere,) * 4,
        scratch_shapes=[
            pltpu.VMEM((ROWS, HEADS * HEAD), BF),
            pltpu.VMEM((ROWS, HEAD), BF),
            pltpu.VMEM((ROWS, HEAD), BF),
            pltpu.VMEM((ROWS, HEADS * HEAD), BF),
            pltpu.VMEM((ROWS,), jnp.int32),
            pltpu.VMEM((STACKED, TILE), F32),
            pltpu.VMEM((HEAD, ROWS), BF),
            pltpu.VMEM((HEAD, ROWS), BF),
            pltpu.VMEM((STACKED, HEADS * TILE), BF),
            pltpu.VMEM((ROWS, HEADS * HEAD), BF),
            pltpu.VMEM((ROWS, HEADS * HEAD), BF),
            pltpu.VMEM((ROWS, HEAD), F32),
            pltpu.VMEM((ROWS, HEAD), F32),
            pltpu.VMEM((ROWS, HEAD), BF),
            pltpu.VMEM((ROWS, HEAD), BF),
            dma((4,)),
            dma,
            dma,
        ],
        compiler_params=pltpu.CompilerParams(
            collective_id=0, has_side_effects=True, vmem_limit_bytes=48 * 2**20
        ),
    )(queries, keys, values, output_gradient, doc_start)
    return pl.pallas_call(
        deliver,
        out_shape=tuple(jax.ShapeDtypeStruct(x.shape, x.dtype) for x in results),
        in_specs=[anywhere] * 4,
        out_specs=(hbm,) * 4,
        scratch_shapes=[dma((4,))],
        compiler_params=pltpu.CompilerParams(vmem_limit_bytes=2**20),
    )(*results)


def solution(mesh):
    return jax.shard_map(
        on_device,
        mesh=mesh,
        in_specs=(P("ctx", "tp"), P("ctx", "tp"), P("ctx", "tp"), P("ctx", "tp"), P("ctx")),
        out_specs=(P(("ctx", "tp"), None), P("ctx", "tp"), P("ctx", "tp"), P("ctx", "tp")),
        check_vma=False,
    )
```
